128 devices in a mesh: readout: 16 (over y, x), pos: 8 (over z, core).
Axes of the slice: x: 4, y: 4, z: 4, core: 2. Of those that a mesh axis runs over, the one named last changes fastest.
Arguments:
- frames: float32 [128, 1024, 1024], P('pos', 'readout'), may hold values from 0 to 4
- dark: float32 [1024, 1024], P('readout'), may hold values from 0 to 0.5
- gain: float32 [1024, 1024], P('readout'), may hold values from 0.5 to 1.5
- offsets: int32 [128, 2], P('pos'), may hold values from 0 to 511
- object_field: float32 [2, 8192, 4096], P(None, 'readout', 'pos'), may hold values from -6 to 6
- probe: float32 [2, 512, 512], replicated, may hold values from -6 to 6
Outputs:
- object_new: float32 [2, 8192, 4096], P(None, 'readout', 'pos')
- probe_new: float32 [2, 512, 512], replicated
The draws below stay inside these ranges and needn't reach their ends.
All inputs are finite; a program needn't handle non-finite values.
Results may differ from the reference program's by a relative error of at most 0.0003.
Values sent between devices are 32-bit elements; how exact they have to be, the bound alone decides.
No kernel may reach another device: no remote copies, remote signals or barrier semaphores. Data moves between devices by JAX's collectives and lax.ppermute only.
A program may use at most 576 MiB of HBM per device.

```python
import jax
import jax.numpy as jnp
from jax import lax

DET = 1024
NB = 512
POS_DEV = 1
BATCH = 128
OBJ_H = 8192
OBJ_W = 4096
N_READOUT = 16


def touch_ends(values, stream_key, least, largest):
    dims = values.shape
    spot = [jax.random.randint(jax.random.fold_in(stream_key, axis), (), 0, dims[axis]) for axis in range(len(dims))]
    values = values.at[tuple(spot)].set(least)
    longest = dims.index(max(dims))
    spot[longest] = (spot[longest] + 1) % dims[longest]
    return values.at[tuple(spot)].set(largest)


def level_of(rng, shape, split, least, high):
    def one(dim, blocks):
        draws = jax.random.uniform(jax.random.fold_in(jax.random.fold_in(rng, 6), dim), (blocks,), jnp.float32, least / len(split), high / len(split))
        return jnp.repeat(jnp.exp(draws), shape[dim] // blocks).reshape((-1,) + (1,) * (len(shape) - dim - 1))

    factor_of = one(*split[0])
    for cut in split[1:]:
        factor_of = factor_of * one(*cut)
    return factor_of


def bell_draw(own_key, dims, scale, most, shards=(), kind=jnp.bfloat16):
    values = jax.random.normal(own_key, dims, jnp.float32) * scale
    if len(shards) > 0:
        values = level_of(own_key, dims, shards, -0.22, 0.18) * values
    return jnp.clip(values, min=-most, max=most).astype(kind)


def setup_inputs(seed: int = 0) -> dict:
    key_list = jax.random.split(jax.random.key(seed), 7)
    frames = jnp.clip(4.0 * jax.random.uniform(key_list[0], (BATCH, DET, DET), jnp.float32) ** level_of(key_list[0], (BATCH, DET, DET), ((0, 8), (1, 16)), -0.2, 0.2), 0.0, 4.0)
    dark = jnp.clip(0.5 * jax.random.uniform(key_list[1], (DET, DET), jnp.float32) ** level_of(key_list[1], (DET, DET), ((0, 16),), -0.2, 0.2), 0.0, 0.5)
    gain = jnp.clip(1.0 + 0.1 * jax.random.normal(key_list[2], (DET, DET), jnp.float32), 0.5, 1.5)
    offsets = touch_ends(jax.random.randint(key_list[3], (BATCH, 2), 0, NB), jax.random.fold_in(key_list[3], 1), 0, NB - 1).astype(jnp.int32)
    object_field = bell_draw(key_list[4], (2, OBJ_H, OBJ_W), 1.0, 6.0, ((1, 16), (2, 8)), jnp.float32)
    probe = bell_draw(key_list[5], (2, NB, NB), 1.0, 6.0, (), jnp.float32)
    return dict(frames=frames, dark=dark, gain=gain, offsets=offsets, object_field=object_field, probe=probe)


def dft2(real_part, imag_part, inverse):
    joined = lax.complex(real_part, imag_part)
    if inverse:
        result = jnp.fft.ifft2(joined, norm='ortho')
    else:
        result = jnp.fft.fft2(joined, norm='ortho')
    return (jnp.real(result), jnp.imag(result))

def reference(frames, dark, gain, offsets, object_field, probe):
    side = NB
    padded = jnp.pad(object_field, ((0, 0), (0, side), (0, side)))
    probe_real = probe[0]
    probe_imag = probe[1]

    def visit(carry, position):
        object_grad, probe_grad, energy = carry
        raw_frame = lax.dynamic_index_in_dim(frames, position, 0, keepdims=False)
        corrected = jnp.maximum(raw_frame - dark, 0.0) * gain
        binned = corrected.reshape(side, 2, side, 2).sum(axis=(1, 3))
        amplitude = jnp.sqrt(binned)
        column_owner = position // (N_READOUT * POS_DEV)
        row_owner = position // POS_DEV % N_READOUT
        row_start = (row_owner * side + offsets[position, 0]).astype(jnp.int32)
        col_start = (column_owner * side + offsets[position, 1]).astype(jnp.int32)
        start = (jnp.zeros((), jnp.int32), row_start, col_start)
        patch = lax.dynamic_slice(padded, start, (2, side, side))
        obj_real = patch[0]
        obj_imag = patch[1]
        wave_real = probe_real * obj_real - probe_imag * obj_imag
        wave_imag = probe_real * obj_imag + probe_imag * obj_real
        spec_real, spec_imag = dft2(wave_real, wave_imag, False)
        magnitude = jnp.sqrt(spec_real * spec_real + spec_imag * spec_imag)
        factor = amplitude / jnp.maximum(magnitude, 0.25)
        back_real, back_imag = dft2(spec_real * factor, spec_imag * factor, True)
        delta_real = back_real - wave_real
        delta_imag = back_imag - wave_imag
        grad_real = probe_real * delta_real + probe_imag * delta_imag
        grad_imag = probe_real * delta_imag - probe_imag * delta_real
        term_pair = jnp.stack([grad_real, grad_imag])
        current = lax.dynamic_slice(object_grad, start, (2, side, side))
        object_grad = lax.dynamic_update_slice(object_grad, current + term_pair, start)
        probe_term = jnp.stack([obj_real * delta_real + obj_imag * delta_imag, obj_real * delta_imag - obj_imag * delta_real])
        probe_grad = probe_grad + probe_term
        energy = energy + obj_real * obj_real + obj_imag * obj_imag
        return ((object_grad, probe_grad, energy), None)
    init_carry = (jnp.zeros(padded.shape, jnp.float32), jnp.zeros(probe.shape, jnp.float32), jnp.zeros((side, side), jnp.float32))
    (object_grad, probe_grad, energy), _ = lax.scan(visit, init_carry, jnp.arange(BATCH, dtype=jnp.int32))
    peak_power = jnp.max(probe_real * probe_real + probe_imag * probe_imag)
    object_new = object_field + object_grad[:, :OBJ_H, :OBJ_W] / peak_power
    probe_new = probe + probe_grad / energy
    return (object_new, probe_new)
```

```python
import functools
import math

import jax
import jax.numpy as jnp
import ml_dtypes
import numpy as np
from jax import lax
from jax.experimental import pallas as pl
from jax.experimental.pallas import tpu as pltpu
from jax.sharding import PartitionSpec as P

SIDE = 512
QUARTER = 128
ROWS = 16
COLS = 8
BOTH = ("readout", "pos")
F32 = jnp.float32
BF16 = jnp.bfloat16
VMEM_BYTES = 56 * 1024 * 1024


def split_table(table):
    high = table.astype(ml_dtypes.bfloat16)
    low = (table - high.astype(np.float64)).astype(ml_dtypes.bfloat16)
    return np.stack([high, low])


@functools.cache
def dft_tables():
    index = np.arange(QUARTER)
    tables = []
    for group in range(4):
        product_mod = (index[:, None] * (4 * index[None, :] + group)) % SIDE
        angles = product_mod * (2.0 * math.pi / SIDE)
        cosine = np.cos(angles) / math.sqrt(SIDE)
        sine = np.sin(angles) / math.sqrt(SIDE)
        tables.append(np.block([[cosine, -sine], [sine, cosine]]))
    straight = np.stack([split_table(table) for table in tables])
    turned = np.stack([split_table(table.T) for table in tables])
    return straight, turned


@functools.cache
def pair_table():
    table = np.zeros((2 * SIDE, SIDE), np.float32)
    for group in range(4):
        for place in range(QUARTER):
            for u in range(2):
                table[8 * place + 2 * group + u, group * QUARTER + place] = 1.0
    return table.astype(ml_dtypes.bfloat16)


def split_two(values):
    high = values.astype(BF16)
    low = (values - high.astype(F32)).astype(BF16)
    return high, low


def bin_kernel(scalars, frames, dark, gain, pairs, out, lanes, sums):
    step = pl.program_id(0)
    count = frames.shape[0]
    for n in range(count):
        corrected = jnp.maximum(frames[n] - dark[...], 0.0) * gain[...]
        for t in range(8):
            lanes[8 * n + t] = corrected[:, QUARTER * t : QUARTER * (t + 1)]
        for t in range(8):
            for group in range(4):
                total = lanes[8 * n + t, pl.ds(2 * group, 8, stride=8), :]
                total += lanes[8 * n + t, pl.ds(2 * group + 1, 8, stride=8), :]
                first = 32 * n + 8 * group
                sums[first : first + 8, QUARTER * t : QUARTER * (t + 1)] = total
    values = sums[...]
    high = values.astype(BF16)
    rest = values - high.astype(F32)
    mid = rest.astype(BF16)
    low = (rest - mid.astype(F32)).astype(BF16)
    table = pairs[...]
    binned = jnp.dot(low, table, preferred_element_type=F32)
    binned += jnp.dot(mid, table, preferred_element_type=F32)
    binned += jnp.dot(high, table, preferred_element_type=F32)
    for n in range(count):
        place = lax.rem(step * count + n + scalars[0], ROWS)
        out[place] = binned[32 * n : 32 * n + 32, :]


def bin_frames(flip, frames, dark, gain):
    per_step = 4
    return pl.pallas_call(
        bin_kernel,
        out_shape=jax.ShapeDtypeStruct((ROWS, 32, SIDE), F32),
        grid_spec=pltpu.PrefetchScalarGridSpec(
            num_scalar_prefetch=1,
            grid=(ROWS // per_step,),
            in_specs=[
                pl.BlockSpec((per_step, 64, 2 * SIDE), lambda s, f: (s, 0, 0)),
                pl.BlockSpec((64, 2 * SIDE), lambda s, f: (0, 0)),
                pl.BlockSpec((64, 2 * SIDE), lambda s, f: (0, 0)),
                pl.BlockSpec((2 * SIDE, SIDE), lambda s, f: (0, 0)),
            ],
            out_specs=pl.BlockSpec((ROWS, 32, SIDE), lambda s, f: (0, 0, 0)),
            scratch_shapes=[
                pltpu.VMEM((8 * per_step, 64, QUARTER), F32),
                pltpu.VMEM((32 * per_step, 2 * SIDE), F32),
            ],
        ),
        compiler_params=pltpu.CompilerParams(vmem_limit_bytes=VMEM_BYTES),
        cost_estimate=pl.CostEstimate(flops=2**31, bytes_accessed=6 * 2**20, transcendentals=0),
        name="bin_frames",
    )(flip, frames, dark, gain, jnp.asarray(pair_table()))


def roll_both(values, down, right):
    return pltpu.roll(pltpu.roll(values, down, 0), right, 1)


def roll_kernel(scalars, probe, out, peak):
    real = probe[0]
    imag = probe[1]
    peak[...] = jnp.broadcast_to(jnp.max(real * real + imag * imag, keepdims=True), (8, 128))
    out[0] = roll_both(real, scalars[0], scalars[1])
    out[1] = roll_both(imag, scalars[0], scalars[1])


def roll_probe(offset, probe):
    return pl.pallas_call(
        roll_kernel,
        out_shape=[jax.ShapeDtypeStruct((2, SIDE, SIDE), F32), jax.ShapeDtypeStruct((8, 128), F32)],
        in_specs=[pl.BlockSpec(memory_space=pltpu.SMEM), pl.BlockSpec(memory_space=pltpu.VMEM)],
        out_specs=[pl.BlockSpec(memory_space=pltpu.VMEM)] * 2,
        compiler_params=pltpu.CompilerParams(vmem_limit_bytes=VMEM_BYTES),
        cost_estimate=pl.CostEstimate(flops=2**22, bytes_accessed=4 * 2**20, transcendentals=0),
        name="roll_probe",
    )(offset, probe)


def times_i(pair):
    return -pair[1], pair[0]


def add(one, two):
    return one[0] + two[0], one[1] + two[1]


def sub(one, two):
    return one[0] - two[0], one[1] - two[1]


def butterfly(x0, x1, x2, x3, sign):
    even_sum, even_diff = add(x0, x2), sub(x0, x2)
    odd_sum, odd_diff = add(x1, x3), sub(x1, x3)
    turned = times_i(odd_diff)
    if sign < 0:
        first, third = sub(even_diff, turned), add(even_diff, turned)
    else:
        first, third = add(even_diff, turned), sub(even_diff, turned)
    return add(even_sum, odd_sum), first, sub(even_sum, odd_sum), third


def three_dots(left_high, left_low, right_high, right_low):
    total = jnp.dot(left_high, right_high, preferred_element_type=F32)
    total += jnp.dot(left_high, right_low, preferred_element_type=F32)
    total += jnp.dot(left_low, right_high, preferred_element_type=F32)
    return total


def main_kernel(
    scalars, tile, r0, r1, r2, r3, n0, n1, n2, n3, probe, binned, straight, turned, peak,
    away, kept, sum_away, sum_kept,
    patch, wave, wide, mid_high, mid_low, full,
):
    o0, o1, own_from, own_to, valid, core = (scalars[i] for i in range(6))
    quarters = [slice(QUARTER * a, QUARTER * (a + 1)) for a in range(4)]
    halves = [slice(0, QUARTER), slice(QUARTER, 2 * QUARTER)]
    rights = [r0, r1, r2, r3]
    others = [n0, n1, n2, n3]

    for a in range(4):
        rows = lax.broadcasted_iota(jnp.int32, (QUARTER, SIDE), 0) + QUARTER * a
        cols = lax.broadcasted_iota(jnp.int32, (QUARTER, SIDE), 1)
        own = (rows >= own_from) & (rows < own_to)
        here = cols >= o1
        for part in range(2):
            mine = jnp.where(here, tile[part, quarters[a], :], rights[a][part])
            mine = jnp.where(valid == 1, mine, 0.0)
            patch[part, quarters[a], :] = jnp.where(own, mine, others[a][part])
        obj = patch[0, quarters[a], :], patch[1, quarters[a], :]
        pr = probe[0, quarters[a], :], probe[1, quarters[a], :]
        wave[0, quarters[a], :] = pr[0] * obj[0] - pr[1] * obj[1]
        wave[1, quarters[a], :] = pr[0] * obj[1] + pr[1] * obj[0]
        blocks = [(wave[0, quarters[a], quarters[b]], wave[1, quarters[a], quarters[b]]) for b in range(4)]
        for g, pair in enumerate(butterfly(*blocks, -1)):
            for part in range(2):
                mid_high[g, quarters[a], halves[part]], mid_low[g, quarters[a], halves[part]] = split_two(pair[part])

    for g in range(4):
        out = three_dots(mid_high[g], mid_low[g], straight[g, 0], straight[g, 1])
        wide[0, :, quarters[g]] = out[:, :QUARTER]
        wide[1, :, quarters[g]] = out[:, QUARTER:]

    for b in range(4):
        blocks = [(wide[0, quarters[a], quarters[b]], wide[1, quarters[a], quarters[b]]) for a in range(4)]
        for h, pair in enumerate(butterfly(*blocks, -1)):
            for part in range(2):
                high, low = split_two(pair[part])
                full[h, 0, halves[part], quarters[b]] = high
                full[h, 1, halves[part], quarters[b]] = low

    for h in range(4):
        spec = three_dots(turned[h, 0], turned[h, 1], full[h, 0], full[h, 1])
        real, imag = spec[:QUARTER], spec[QUARTER:]
        power = real * real + imag * imag
        level = binned[:, 8 * h : 8 * h + 8, :].reshape(QUARTER, SIDE)
        factor = jnp.sqrt(level) * lax.rsqrt(jnp.maximum(power, 0.0625))
        for part, value in enumerate((real * factor, imag * factor)):
            high, low = split_two(value)
            full[h, 0, halves[part], :] = high
            full[h, 1, halves[part], :] = low

    for h in range(4):
        back = three_dots(straight[h, 0], straight[h, 1], full[h, 0], full[h, 1])
        wide[0, quarters[h], :] = back[:QUARTER]
        wide[1, quarters[h], :] = back[QUARTER:]

    for b in range(4):
        blocks = [(wide[0, quarters[h], quarters[b]], wide[1, quarters[h], quarters[b]]) for h in range(4)]
        for a, pair in enumerate(butterfly(*blocks, 1)):
            for part in range(2):
                mid_high[b, quarters[a], halves[part]], mid_low[b, quarters[a], halves[part]] = split_two(pair[part])

    for g in range(4):
        out = three_dots(mid_high[g], mid_low[g], turned[g, 0], turned[g, 1])
        wide[0, :, quarters[g]] = out[:, :QUARTER]
        wide[1, :, quarters[g]] = out[:, QUARTER:]

    scale = 1.0 / peak[0:1, 0:1]
    for a in range(4):
        rows = lax.broadcasted_iota(jnp.int32, (QUARTER, QUARTER), 0) + QUARTER * a
        own = (rows >= own_from) & (rows < own_to)
        keep = own & (valid == 1)
        blocks = [(wide[0, quarters[a], quarters[g]], wide[1, quarters[a], quarters[g]]) for g in range(4)]
        for b, back in enumerate(butterfly(*blocks, 1)):
            at = (quarters[a], quarters[b])
            dr = back[0] - wave[0, at[0], at[1]]
            di = back[1] - wave[1, at[0], at[1]]
            pr, pi = probe[0, at[0], at[1]], probe[1, at[0], at[1]]
            grad = (pr * dr + pi * di) * scale, (pr * di - pi * dr) * scale
            for part in range(2):
                kept[part, at[0], at[1]] = jnp.where(keep, grad[part], 0.0)
                away[part, at[0], at[1]] = jnp.where(own, 0.0, grad[part])
            cr, ci = patch[0, at[0], at[1]], patch[1, at[0], at[1]]
            wide[0, at[0], at[1]] = cr * dr + ci * di
            wide[1, at[0], at[1]] = cr * di - ci * dr
            wide[2, at[0], at[1]] = cr * cr + ci * ci

    up = lax.rem(SIDE - o0, SIDE)
    left = lax.rem(SIDE - o1, SIDE)
    half = SIDE // 2
    for part in range(3):
        wide[part] = roll_both(wide[part], up, left)
        sum_kept[part] = wide[part, pl.ds(pl.multiple_of(core * half, half), half), :]
        sum_away[part] = wide[part, pl.ds(pl.multiple_of((1 - core) * half, half), half), :]


def main_call(scalars, tile, rights, others, probe, binned, peak):
    straight, turned = dft_tables()
    whole = (2, SIDE, SIDE)
    half = (3, SIDE // 2, SIDE)
    vmem = pl.BlockSpec(memory_space=pltpu.VMEM)
    return pl.pallas_call(
        main_kernel,
        out_shape=[jax.ShapeDtypeStruct(s, F32) for s in (whole, whole, half, half)],
        in_specs=[pl.BlockSpec(memory_space=pltpu.SMEM)] + [vmem] * 14,
        out_specs=[vmem] * 4,
        scratch_shapes=[
            pltpu.VMEM(whole, F32),
            pltpu.VMEM(whole, F32),
            pltpu.VMEM((3, SIDE, SIDE), F32),
            pltpu.VMEM((4, SIDE, 2 * QUARTER), BF16),
            pltpu.VMEM((4, SIDE, 2 * QUARTER), BF16),
            pltpu.VMEM((4, 2, 2 * QUARTER, SIDE), BF16),
        ],
        compiler_params=pltpu.CompilerParams(vmem_limit_bytes=VMEM_BYTES),
        cost_estimate=pl.CostEstimate(flops=8 * 2**30, bytes_accessed=20 * 2**20, transcendentals=2**19),
        name="phase_update",
    )(scalars, tile, *rights, *others, probe, binned, jnp.asarray(straight), jnp.asarray(turned), peak)


def send(block, axis, route):
    return lax.ppermute(block, axis, route)


def device_pairs(move):
    pairs = []
    for r in range(ROWS):
        for p in range(COLS):
            target = move(r, p)
            if target is not None:
                pairs.append((r * COLS + p, target[0] * COLS + target[1]))
    return pairs


def gather_pairs(r, p):
    if p % 2 == 0:
        return (r - 1, p) if r > 0 else None
    return ((r + 1) % ROWS, p)


def scatter_pairs(r, p):
    if p % 2 == 0:
        return (r + 1, p) if r < ROWS - 1 else None
    return ((r - 1) % ROWS, p)


def ring_z(distance):
    return [(p, (p + 2 * distance) % COLS) for p in range(COLS)]


def ring_y(distance):
    return [(r, (r + 4 * distance) % ROWS) for r in range(ROWS)]


def ring_x(distance):
    return [(r, r // 4 * 4 + (r + distance) % 4) for r in range(ROWS)]


def scatter_sum(values, axis, ring, place):
    size = values.shape[1] // 4

    def piece(distance):
        start = lax.rem(place + distance, 4) * size
        return lax.dynamic_slice_in_dim(values, start, size, 1)

    parts = [send(piece(k), axis, ring(k)) for k in (2, 1, 3)]
    return (piece(0) + parts[0]) + (parts[1] + parts[2])


def gather_all(values, axis, ring, place):
    size = values.shape[1]
    parts = {k: send(values, axis, ring(k)) for k in (2, 1, 3)}
    out = jnp.zeros((values.shape[0], 4 * size, values.shape[2]), F32)
    out = lax.dynamic_update_slice_in_dim(out, values, place * size, 1)
    for k, part in parts.items():
        out = lax.dynamic_update_slice_in_dim(out, part, lax.rem(place - k + 4, 4) * size, 1)
    return out


def on_device(frames, dark, gain, offsets, object_field, probe):
    r = lax.axis_index("readout")
    p = lax.axis_index("pos")
    flip = lax.rem(p, 2)
    z = p // 2
    x, y = lax.rem(r, 4), r // 4
    position = lax.rem(r - flip + ROWS, ROWS)
    beside = lax.rem(r - 1 + flip + ROWS, ROWS)
    o0 = offsets[position, 0]
    o1 = offsets[position, 1]
    o1_beside = offsets[beside, 1]
    own_from = jnp.where(flip == 1, 0, o0)
    own_to = jnp.where(flip == 1, o0, SIDE)
    valid = jnp.where((flip == 1) & (r == 0), 0, 1)
    scalars = jnp.stack([o0, o1, own_from, own_to, valid, flip]).astype(jnp.int32)

    to_left = [(i, i - 1) for i in range(1, COLS)]
    to_right = [(i, i + 1) for i in range(COLS - 1)]
    chunks = [object_field[:, QUARTER * a : QUARTER * (a + 1)] for a in range(4)]
    rights = [send(chunk, "pos", to_left) for chunk in chunks]
    binned = bin_frames(flip[None].astype(jnp.int32), frames, dark, gain)
    regrouped = lax.all_to_all(binned, "readout", split_axis=0, concat_axis=0, tiled=True)
    cols = lax.broadcasted_iota(jnp.int32, (2, QUARTER, SIDE), 2)
    joined = [jnp.where(cols >= o1_beside, chunks[a], rights[a]) for a in range(4)]
    others = [send(block, BOTH, device_pairs(gather_pairs)) for block in joined]
    rolled, peak = roll_probe(scalars, probe)

    away, kept, sum_away, sum_kept = main_call(scalars, object_field, rights, others, rolled, regrouped, peak)

    swapped = send(sum_away, "pos", [(i, i ^ 1) for i in range(COLS)])
    arrived = [
        send(away[:, QUARTER * a : QUARTER * (a + 1)], BOTH, device_pairs(scatter_pairs)) for a in range(4)
    ]
    news = []
    for a in range(4):
        mine = kept[:, QUARTER * a : QUARTER * (a + 1)]
        outward = jnp.where(cols < o1, mine, 0.0) + jnp.where(cols < o1_beside, arrived[a], 0.0)
        landed = send(outward, "pos", to_right)
        inward = jnp.where(cols >= o1, mine, 0.0) + jnp.where(cols >= o1_beside, arrived[a], 0.0)
        news.append(chunks[a] + (inward + landed))
    object_new = jnp.concatenate(news, axis=1)

    total = sum_kept + swapped
    total = scatter_sum(total, "pos", ring_z, z)
    total = scatter_sum(total, "readout", ring_y, y)
    parts = [send(total, "readout", ring_x(k)) for k in (2, 1, 3)]
    total = (total + parts[0]) + (parts[1] + parts[2])
    start = flip * (SIDE // 2) + z * (SIDE // 8) + y * (SIDE // 32)
    own_probe = lax.dynamic_slice_in_dim(probe, start, SIDE // 32, 1)
    piece = own_probe + total[:2] / total[2:]
    piece = gather_all(piece, "readout", ring_y, y)
    piece = gather_all(piece, "pos", ring_z, z)
    other = send(piece, "pos", [(i, i ^ 1) for i in range(COLS)])
    first = jnp.where(flip == 0, piece, other)
    second = jnp.where(flip == 0, other, piece)
    probe_new = jnp.concatenate([first, second], axis=1)
    return (object_new, probe_new)


def solution(mesh):
    in_specs = (
        P("pos", "readout", None),
        P("readout", None),
        P("readout", None),
        P("pos", None),
        P(None, "readout", "pos"),
        P(),
    )
    out_specs = (P(None, "readout", "pos"), P())
    return jax.shard_map(
        on_device, mesh=mesh, in_specs=in_specs, out_specs=out_specs, check_vma=False
    )
```

```python
import functools
import math

import jax
import jax.numpy as jnp
import ml_dtypes
import numpy as np
from jax import lax
from jax.experimental import pallas as pl
from jax.experimental.pallas import tpu as pltpu
from jax.sharding import PartitionSpec as P

SIDE = 512
QUARTER = 128
ROWS = 16
COLS = 8
STRIP = 16
CUT = 320
BOTH = ("readout", "pos")
F32 = jnp.float32
BF16 = jnp.bfloat16
VMEM_BYTES = 56 * 1024 * 1024


def split_table(table):
    high = table.astype(ml_dtypes.bfloat16)
    low = (table - high.astype(np.float64)).astype(ml_dtypes.bfloat16)
    return np.stack([high, low])


@functools.cache
def dft_tables():
    index = np.arange(QUARTER)
    tables = []
    for group in range(4):
        product_mod = (index[:, None] * (4 * index[None, :] + group)) % SIDE
        angles = product_mod * (2.0 * math.pi / SIDE)
        cosine = np.cos(angles) / math.sqrt(SIDE)
        sine = np.sin(angles) / math.sqrt(SIDE)
        tables.append(np.block([[cosine, -sine], [sine, cosine]]))
    straight = np.stack([split_table(table) for table in tables])
    turned = np.stack([split_table(table.T) for table in tables])
    return straight, turned


@functools.cache
def pair_table():
    table = np.zeros((2 * SIDE, SIDE), np.float32)
    for group in range(4):
        for place in range(QUARTER):
            for u in range(2):
                table[8 * place + 2 * group + u, group * QUARTER + place] = 1.0
    return table.astype(ml_dtypes.bfloat16)


def my_place():
    r = lax.axis_index("readout")
    p = lax.axis_index("pos")
    return r, lax.rem(r, 4), r // 4, p // 2, lax.rem(p, 2)


def split_two(values):
    high = values.astype(BF16)
    low = (values - high.astype(F32)).astype(BF16)
    return high, low


def bin_kernel(frames, dark, gain, pairs, out, lanes, sums):
    step = pl.program_id(0)
    flip = my_place()[4]
    count = frames.shape[0]
    for n in range(count):
        corrected = jnp.maximum(frames[n] - dark[...], 0.0) * gain[...]
        for t in range(8):
            lanes[8 * n + t] = corrected[:, QUARTER * t : QUARTER * (t + 1)]
        for t in range(8):
            for group in range(4):
                total = lanes[8 * n + t, pl.ds(2 * group, 8, stride=8), :]
                total += lanes[8 * n + t, pl.ds(2 * group + 1, 8, stride=8), :]
                first = 32 * n + 8 * group
                sums[first : first + 8, QUARTER * t : QUARTER * (t + 1)] = total
    values = sums[...]
    high = values.astype(BF16)
    rest = values - high.astype(F32)
    mid = rest.astype(BF16)
    low = (rest - mid.astype(F32)).astype(BF16)
    table = pairs[...]
    binned = jnp.dot(low, table, preferred_element_type=F32)
    binned += jnp.dot(mid, table, preferred_element_type=F32)
    binned += jnp.dot(high, table, preferred_element_type=F32)
    for n in range(count):
        place = lax.rem(step * count + n + flip, ROWS)
        out[place] = binned[32 * n : 32 * n + 32, :]


def bin_frames(frames, dark, gain):
    per_step = 8
    return pl.pallas_call(
        bin_kernel,
        out_shape=jax.ShapeDtypeStruct((ROWS, 32, SIDE), F32),
        grid=(ROWS // per_step,),
        in_specs=[
            pl.BlockSpec((per_step, 64, 2 * SIDE), lambda s: (s, 0, 0)),
            pl.BlockSpec((64, 2 * SIDE), lambda s: (0, 0)),
            pl.BlockSpec((64, 2 * SIDE), lambda s: (0, 0)),
            pl.BlockSpec((2 * SIDE, SIDE), lambda s: (0, 0)),
        ],
        out_specs=pl.BlockSpec((ROWS, 32, SIDE), lambda s: (0, 0, 0)),
        scratch_shapes=[
            pltpu.VMEM((8 * per_step, 64, QUARTER), F32),
            pltpu.VMEM((32 * per_step, 2 * SIDE), F32),
        ],
        compiler_params=pltpu.CompilerParams(vmem_limit_bytes=VMEM_BYTES),
        cost_estimate=pl.CostEstimate(flops=0, bytes_accessed=0, transcendentals=0),
        name="bin_frames",
    )(frames, dark, gain, jnp.asarray(pair_table()))


def roll_both(values, down, right):
    return pltpu.roll(pltpu.roll(values, down, 0), right, 1)


def roll_kernel(offsets, probe, out, peak):
    r, _, _, _, flip = my_place()
    position = lax.rem(r - flip + ROWS, ROWS)
    o0, o1 = offsets[position, 0], offsets[position, 1]
    real = probe[0]
    imag = probe[1]
    peak[...] = jnp.broadcast_to(jnp.max(real * real + imag * imag, keepdims=True), (8, 128))
    out[0] = roll_both(real, o0, o1)
    out[1] = roll_both(imag, o0, o1)


def roll_probe(offset, probe):
    return pl.pallas_call(
        roll_kernel,
        out_shape=[jax.ShapeDtypeStruct((2, SIDE, SIDE), F32), jax.ShapeDtypeStruct((8, 128), F32)],
        in_specs=[pl.BlockSpec(memory_space=pltpu.SMEM), pl.BlockSpec(memory_space=pltpu.VMEM)],
        out_specs=[pl.BlockSpec(memory_space=pltpu.VMEM)] * 2,
        compiler_params=pltpu.CompilerParams(vmem_limit_bytes=VMEM_BYTES),
        cost_estimate=pl.CostEstimate(flops=2**22, bytes_accessed=64 * 2**20, transcendentals=0),
        name="roll_probe",
    )(offset, probe)


def times_i(pair):
    return -pair[1], pair[0]


def add(one, two):
    return one[0] + two[0], one[1] + two[1]


def sub(one, two):
    return one[0] - two[0], one[1] - two[1]


def butterfly(x0, x1, x2, x3, sign):
    even_sum, even_diff = add(x0, x2), sub(x0, x2)
    odd_sum, odd_diff = add(x1, x3), sub(x1, x3)
    turned = times_i(odd_diff)
    if sign < 0:
        first, third = sub(even_diff, turned), add(even_diff, turned)
    else:
        first, third = add(even_diff, turned), sub(even_diff, turned)
    return add(even_sum, odd_sum), first, sub(even_sum, odd_sum), third


def three_dots(left_high, left_low, right_high, right_low):
    total = jnp.dot(left_high, right_high, preferred_element_type=F32)
    total += jnp.dot(left_high, right_low, preferred_element_type=F32)
    total += jnp.dot(left_low, right_high, preferred_element_type=F32)
    return total


def strip_rows(core, z, y):
    start = core * (SIDE // 2) + lax.rem(z, 4) * (SIDE // 8) + lax.rem(y, 4) * STRIP
    return pl.ds(pl.multiple_of(start, STRIP), STRIP)


def main_kernel(
    offsets, tile_hbm, r0_hbm, r1_hbm, n0_hbm, n1_hbm, probe_hbm, binned_hbm, straight_hbm, turned_hbm, peak,
    change, sum_away, sum_kept,
    patch, wave, wide, mid_high, mid_low, full, tile, right, other, probe, binned, straight, turned, sems,
):
    r, _, y, z, core = my_place()
    position = lax.rem(r - core + ROWS, ROWS)
    o0, o1 = offsets[position, 0], offsets[position, 1]
    own_from = jnp.where(core == 1, 0, o0)
    own_to = jnp.where(core == 1, o0, SIDE)
    valid = jnp.where((core == 1) & (r == 0), 0, 1)
    quarters = [slice(QUARTER * a, QUARTER * (a + 1)) for a in range(4)]
    halves = [slice(0, QUARTER), slice(QUARTER, 2 * QUARTER)]

    early, late = [], []

    def fetch(group, source, target):
        copy = pltpu.make_async_copy(source, target, sems.at[len(early) + len(late)])
        copy.start()
        group.append(copy)

    for source0, source1, target in ((r0_hbm, r1_hbm, right), (n0_hbm, n1_hbm, other)):
        fetch(early, source0, target.at[:, :CUT])
        fetch(early, source1, target.at[:, CUT:])
    for piece in (slice(0, SIDE // 2), slice(SIDE // 2, SIDE)):
        fetch(early, tile_hbm.at[:, piece], tile.at[:, piece])
        fetch(early, probe_hbm.at[:, piece], probe.at[:, piece])
    fetch(late, straight_hbm, straight)
    fetch(late, turned_hbm, turned)
    fetch(late, binned_hbm, binned)
    step = QUARTER // 2
    for n in range(8):
        if n == 0:
            for k in (0, 2, 4, 5):
                early[k].wait()
        if n == 4:
            for k in (1, 3, 6, 7):
                early[k].wait()
        piece = slice(step * n, step * (n + 1))
        rows = lax.broadcasted_iota(jnp.int32, (step, SIDE), 0) + step * n
        cols = lax.broadcasted_iota(jnp.int32, (step, SIDE), 1)
        own = (rows >= own_from) & (rows < own_to)
        here = cols >= o1
        obj = []
        for part in range(2):
            mine = jnp.where(here, tile[part, piece, :], right[part, piece, :])
            mine = jnp.where(valid == 1, mine, 0.0)
            obj.append(jnp.where(own, mine, other[part, piece, :]))
            patch[part, piece, :] = obj[part]
        pr = probe[0, piece, :], probe[1, piece, :]
        wave[0, piece, :] = pr[0] * obj[0] - pr[1] * obj[1]
        wave[1, piece, :] = pr[0] * obj[1] + pr[1] * obj[0]
    for a in range(4):
        blocks = [(wave[0, quarters[a], quarters[b]], wave[1, quarters[a], quarters[b]]) for b in range(4)]
        for g, pair in enumerate(butterfly(*blocks, -1)):
            for part in range(2):
                mid_high[g, quarters[a], halves[part]], mid_low[g, quarters[a], halves[part]] = split_two(pair[part])

    late[0].wait()
    for g in range(4):
        out = three_dots(mid_high[g], mid_low[g], straight[g, 0], straight[g, 1])
        wide[0, :, quarters[g]] = out[:, :QUARTER]
        wide[1, :, quarters[g]] = out[:, QUARTER:]

    for b in range(4):
        blocks = [(wide[0, quarters[a], quarters[b]], wide[1, quarters[a], quarters[b]]) for a in range(4)]
        for h, pair in enumerate(butterfly(*blocks, -1)):
            for part in range(2):
                high, low = split_two(pair[part])
                full[h, 0, halves[part], quarters[b]] = high
                full[h, 1, halves[part], quarters[b]] = low

    late[1].wait()
    late[2].wait()
    for h in range(4):
        spec = three_dots(turned[h, 0], turned[h, 1], full[h, 0], full[h, 1])
        real, imag = spec[:QUARTER], spec[QUARTER:]
        power = real * real + imag * imag
        level = binned[:, 8 * h : 8 * h + 8, :].reshape(QUARTER, SIDE)
        factor = jnp.sqrt(level) * lax.rsqrt(jnp.maximum(power, 0.0625))
        for part, value in enumerate((real * factor, imag * factor)):
            high, low = split_two(value)
            full[h, 0, halves[part], :] = high
            full[h, 1, halves[part], :] = low

    for h in range(4):
        back = three_dots(straight[h, 0], straight[h, 1], full[h, 0], full[h, 1])
        wide[0, quarters[h], :] = back[:QUARTER]
        wide[1, quarters[h], :] = back[QUARTER:]

    for b in range(4):
        blocks = [(wide[0, quarters[h], quarters[b]], wide[1, quarters[h], quarters[b]]) for h in range(4)]
        for a, pair in enumerate(butterfly(*blocks, 1)):
            for part in range(2):
                mid_high[b, quarters[a], halves[part]], mid_low[b, quarters[a], halves[part]] = split_two(pair[part])

    for g in range(4):
        out = three_dots(mid_high[g], mid_low[g], turned[g, 0], turned[g, 1])
        wide[0, :, quarters[g]] = out[:, :QUARTER]
        wide[1, :, quarters[g]] = out[:, QUARTER:]

    scale = 1.0 / peak[0:1, 0:1]
    for a in range(4):
        blocks = [(wide[0, quarters[a], quarters[g]], wide[1, quarters[a], quarters[g]]) for g in range(4)]
        for b, back in enumerate(butterfly(*blocks, 1)):
            at = (quarters[a], quarters[b])
            dr = back[0] - wave[0, at[0], at[1]]
            di = back[1] - wave[1, at[0], at[1]]
            pr, pi = probe[0, at[0], at[1]], probe[1, at[0], at[1]]
            change[0, at[0], at[1]] = (pr * dr + pi * di) * scale
            change[1, at[0], at[1]] = (pr * di - pi * dr) * scale
            cr, ci = patch[0, at[0], at[1]], patch[1, at[0], at[1]]
            wide[0, at[0], at[1]] = cr * dr + ci * di
            wide[1, at[0], at[1]] = cr * di - ci * dr
            wide[2, at[0], at[1]] = cr * cr + ci * ci

    up = lax.rem(SIDE - o0, SIDE)
    left = lax.rem(SIDE - o1, SIDE)
    for part in range(3):
        wide[part] = roll_both(wide[part], up, left)
        for i in range(4):
            for j in range(4):
                sum_kept[i, j, part] = wide[part, strip_rows(core, z + i, y + j), :]
                sum_away[i, j, part] = wide[part, strip_rows(1 - core, z + i, y + j), :]


def main_call(offsets, tile, rights, others, probe, binned, peak):
    straight, turned = dft_tables()
    whole = (2, SIDE, SIDE)
    half = (4, 4, 3, STRIP, SIDE)
    vmem = pl.BlockSpec(memory_space=pltpu.VMEM)
    anywhere = pl.BlockSpec(memory_space=pl.ANY)
    tables = (4, 2, 2 * QUARTER, 2 * QUARTER)
    return pl.pallas_call(
        main_kernel,
        out_shape=[jax.ShapeDtypeStruct(s, F32) for s in (whole, half, half)],
        in_specs=[pl.BlockSpec(memory_space=pltpu.SMEM)] + [anywhere] * 9 + [vmem],
        out_specs=[vmem] * 3,
        scratch_shapes=[
            pltpu.VMEM(whole, F32),
            pltpu.VMEM(whole, F32),
            pltpu.VMEM((3, SIDE, SIDE), F32),
            pltpu.VMEM((4, SIDE, 2 * QUARTER), BF16),
            pltpu.VMEM((4, SIDE, 2 * QUARTER), BF16),
            pltpu.VMEM((4, 2, 2 * QUARTER, SIDE), BF16),
            pltpu.VMEM(whole, F32),
            pltpu.VMEM(whole, F32),
            pltpu.VMEM(whole, F32),
            pltpu.VMEM(whole, F32),
            pltpu.VMEM((ROWS, 32, SIDE), F32),
            pltpu.VMEM(tables, BF16),
            pltpu.VMEM(tables, BF16),
            pltpu.SemaphoreType.DMA((11,)),
        ],
        compiler_params=pltpu.CompilerParams(vmem_limit_bytes=VMEM_BYTES),
        cost_estimate=pl.CostEstimate(flops=8 * 2**30, bytes_accessed=20 * 2**20, transcendentals=2**19),
        name="phase_update",
    )(offsets, tile, *rights, *others, probe, binned, jnp.asarray(straight), jnp.asarray(turned), peak)


def send(block, axis, route):
    return lax.ppermute(block, axis, route)


def device_pairs(move):
    pairs = []
    for r in range(ROWS):
        for p in range(COLS):
            target = move(r, p)
            if target is not None:
                pairs.append((r * COLS + p, target[0] * COLS + target[1]))
    return pairs


def gather_pairs(r, p):
    if p % 2 == 0:
        return (r - 1, p) if r > 0 else None
    return ((r + 1) % ROWS, p)


def scatter_pairs(r, p):
    if p % 2 == 0:
        return (r + 1, p) if r < ROWS - 1 else None
    return ((r - 1) % ROWS, p)


def ring_z(distance):
    return [(p, (p + 2 * distance) % COLS) for p in range(COLS)]


def ring_y(distance):
    return [(r, (r + 4 * distance) % ROWS) for r in range(ROWS)]


def ring_x(distance):
    return [(r, r // 4 * 4 + (r + distance) % 4) for r in range(ROWS)]


def around(values, axis, ring):
    return [send(values, axis, ring(k)) for k in (1, 2, 3)]


def scatter_sum(values, axis, ring):
    first, second, third = (send(values[k], axis, ring(k)) for k in (1, 2, 3))
    return (values[0] + second) + (first + third)


def place_kernel(o0, o1, o2, o3, other, out):
    _, _, y, z, core = my_place()
    for i, own in enumerate((o0, o1, o2, o3)):
        for j in range(4):
            for part in range(2):
                out[part, strip_rows(core, z + 4 - i, y + 4 - j), :] = own[j, part]
                out[part, strip_rows(1 - core, z + 4 - i, y + 4 - j), :] = other[i, j, part]


def place_strips(own, other):
    vmem = pl.BlockSpec(memory_space=pltpu.VMEM)
    return pl.pallas_call(
        place_kernel,
        out_shape=jax.ShapeDtypeStruct((2, SIDE, SIDE), F32),
        in_specs=[vmem] * 5,
        out_specs=vmem,
        compiler_params=pltpu.CompilerParams(vmem_limit_bytes=VMEM_BYTES),
        cost_estimate=pl.CostEstimate(flops=0, bytes_accessed=4 * 2**20, transcendentals=0),
        name="place_strips",
    )(*own, other)


def on_device(frames, dark, gain, offsets, object_field, probe):
    r = lax.axis_index("readout")
    p = lax.axis_index("pos")
    flip = lax.rem(p, 2)
    z = p // 2
    x, y = lax.rem(r, 4), r // 4
    position = lax.rem(r - flip + ROWS, ROWS)
    beside = lax.rem(r - 1 + flip + ROWS, ROWS)
    o1 = offsets[position, 1]
    o1_beside = offsets[beside, 1]

    to_left = [(i, i - 1) for i in range(1, COLS)]
    to_right = [(i, i + 1) for i in range(COLS - 1)]
    swap_cores = [(i, i ^ 1) for i in range(COLS)]
    half = SIDE // 2
    chunks = [object_field[:, :CUT], object_field[:, CUT:]]
    chunks = lax.optimization_barrier(chunks)
    rights = [send(chunk, "pos", to_left) for chunk in chunks]
    binned = bin_frames(frames, dark, gain)
    cols = lax.broadcasted_iota(jnp.int32, (2, SIDE, SIDE), 2)
    regrouped = lax.all_to_all(binned, "readout", split_axis=0, concat_axis=0, tiled=True)
    joined = []
    for a in range(2):
        before = (joined[0], regrouped) if a > 0 else binned
        rights[a], _ = lax.optimization_barrier((rights[a], before))
        joined.append(jnp.where(cols[:, : chunks[a].shape[1]] >= o1_beside, chunks[a], rights[a]))
    others = [send(block, BOTH, device_pairs(gather_pairs)) for block in joined]
    rolled, peak = roll_probe(offsets, probe)

    change, sum_away, sum_kept = main_call(offsets, object_field, rights, others, rolled, regrouped, peak)

    rows = lax.broadcasted_iota(jnp.int32, (2, SIDE, SIDE), 1)
    upper, upper_beside = rows >= offsets[position, 0], rows >= offsets[beside, 0]
    mine = ((flip == 0) & upper) | ((flip == 1) & (r > 0) & ~upper)
    theirs = ((flip == 0) & ~upper_beside) | ((flip == 1) & upper_beside)

    def landing(inside, inside_beside):
        return jnp.where(mine & inside, change, 0.0) + jnp.where(theirs & inside_beside, arrived, 0.0)

    arrived = send(change, BOTH, device_pairs(scatter_pairs))
    total = sum_kept + send(sum_away, "pos", swap_cores)
    total = scatter_sum(total, "pos", ring_z)
    total, arrived = lax.optimization_barrier((total, arrived))
    total, outward = lax.optimization_barrier((total, landing(cols < o1, cols < o1_beside)))
    landed = send(outward, "pos", to_right)
    total = scatter_sum(total, "readout", ring_y)
    first, second, third = around(total, "readout", ring_x)
    total = (total + second) + (first + third)
    start = flip * half + z * (SIDE // 8) + y * STRIP
    piece = lax.dynamic_slice_in_dim(probe, start, STRIP, 1) + total[:2] / total[2:]
    strips = jnp.stack([piece] + around(piece, "readout", ring_y))
    change, arrived, _ = lax.optimization_barrier((change, arrived, strips))
    inward = object_field + landing(cols >= o1, cols >= o1_beside)
    own = [strips] + around(strips, "pos", ring_z)
    own, landed, inward = lax.optimization_barrier((own, landed, inward))
    object_new = inward + landed
    other = send(jnp.stack(own), "pos", swap_cores)
    probe_new = place_strips(own, other)
    return (object_new, probe_new)


def solution(mesh):
    in_specs = (
        P("pos", "readout", None),
        P("readout", None),
        P("readout", None),
        P("pos", None),
        P(None, "readout", "pos"),
        P(),
    )
    out_specs = (P(None, "readout", "pos"), P())
    return jax.shard_map(
        on_device, mesh=mesh, in_specs=in_specs, out_specs=out_specs, check_vma=False
    )
```

```python
import functools
import math

import jax
import jax.numpy as jnp
import ml_dtypes
import numpy as np
from jax import lax
from jax.experimental import pallas as pl
from jax.experimental.pallas import tpu as pltpu
from jax.sharding import PartitionSpec as P

SIDE = 512
QUARTER = 128
ROWS = 16
COLS = 8
STRIP = 16
CUT = 320
BOTH = ("readout", "pos")
F32 = jnp.float32
BF16 = jnp.bfloat16
VMEM_BYTES = 56 * 1024 * 1024


def split_table(table):
    high = table.astype(ml_dtypes.bfloat16)
    low = (table - high.astype(np.float64)).astype(ml_dtypes.bfloat16)
    return np.stack([high, low])


@functools.cache
def dft_tables():
    index = np.arange(QUARTER)
    tables = []
    for group in range(4):
        product_mod = (index[:, None] * (4 * index[None, :] + group)) % SIDE
        angles = product_mod * (2.0 * math.pi / SIDE)
        cosine = np.cos(angles) / math.sqrt(SIDE)
        sine = np.sin(angles) / math.sqrt(SIDE)
        tables.append(np.block([[cosine, -sine], [sine, cosine]]))
    straight = np.stack([split_table(table) for table in tables])
    turned = np.stack([split_table(table.T) for table in tables])
    return straight, turned


@functools.cache
def pair_table():
    table = np.zeros((2 * SIDE, SIDE), np.float32)
    for group in range(4):
        for place in range(QUARTER):
            for u in range(2):
                table[8 * place + 2 * group + u, group * QUARTER + place] = 1.0
    return table.astype(ml_dtypes.bfloat16)


def my_place():
    r = lax.axis_index("readout")
    p = lax.axis_index("pos")
    return r, lax.rem(r, 4), r // 4, p // 2, lax.rem(p, 2)


def split_two(values):
    high = values.astype(BF16)
    low = (values - high.astype(F32)).astype(BF16)
    return high, low


def bin_kernel(frames, dark, gain, pairs, out, lanes, sums):
    step = pl.program_id(0)
    flip = my_place()[4]
    count = frames.shape[0]
    for n in range(count):
        corrected = jnp.maximum(frames[n] - dark[...], 0.0) * gain[...]
        for t in range(8):
            lanes[8 * n + t] = corrected[:, QUARTER * t : QUARTER * (t + 1)]
        for t in range(8):
            for group in range(4):
                total = lanes[8 * n + t, pl.ds(2 * group, 8, stride=8), :]
                total += lanes[8 * n + t, pl.ds(2 * group + 1, 8, stride=8), :]
                first = 32 * n + 8 * group
                sums[first : first + 8, QUARTER * t : QUARTER * (t + 1)] = total
    values = sums[...]
    high, low = split_two(values)
    table = pairs[...]
    binned = jnp.dot(low, table, preferred_element_type=F32)
    binned += jnp.dot(high, table, preferred_element_type=F32)
    for n in range(count):
        place = lax.rem(step * count + n + flip, ROWS)
        out[place] = binned[32 * n : 32 * n + 32, :]


def bin_frames(frames, dark, gain):
    per_step = 8
    return pl.pallas_call(
        bin_kernel,
        out_shape=jax.ShapeDtypeStruct((ROWS, 32, SIDE), F32),
        grid=(ROWS // per_step,),
        in_specs=[
            pl.BlockSpec((per_step, 64, 2 * SIDE), lambda s: (s, 0, 0)),
            pl.BlockSpec((64, 2 * SIDE), lambda s: (0, 0)),
            pl.BlockSpec((64, 2 * SIDE), lambda s: (0, 0)),
            pl.BlockSpec((2 * SIDE, SIDE), lambda s: (0, 0)),
        ],
        out_specs=pl.BlockSpec((ROWS, 32, SIDE), lambda s: (0, 0, 0)),
        scratch_shapes=[
            pltpu.VMEM((8 * per_step, 64, QUARTER), F32),
            pltpu.VMEM((32 * per_step, 2 * SIDE), F32),
        ],
        compiler_params=pltpu.CompilerParams(vmem_limit_bytes=VMEM_BYTES),
        cost_estimate=pl.CostEstimate(flops=0, bytes_accessed=0, transcendentals=0),
        name="bin_frames",
    )(frames, dark, gain, jnp.asarray(pair_table()))


def roll_both(values, down, right):
    return pltpu.roll(pltpu.roll(values, down, 0), right, 1)


def roll_kernel(offsets, probe, out, peak):
    r, _, _, _, flip = my_place()
    position = lax.rem(r - flip + ROWS, ROWS)
    o0, o1 = offsets[position, 0], offsets[position, 1]
    real = probe[0]
    imag = probe[1]
    peak[...] = jnp.broadcast_to(jnp.max(real * real + imag * imag, keepdims=True), (8, 128))
    out[0] = roll_both(real, o0, o1)
    out[1] = roll_both(imag, o0, o1)


def roll_probe(offset, probe):
    return pl.pallas_call(
        roll_kernel,
        out_shape=[jax.ShapeDtypeStruct((2, SIDE, SIDE), F32), jax.ShapeDtypeStruct((8, 128), F32)],
        in_specs=[pl.BlockSpec(memory_space=pltpu.SMEM), pl.BlockSpec(memory_space=pltpu.VMEM)],
        out_specs=[pl.BlockSpec(memory_space=pltpu.VMEM)] * 2,
        compiler_params=pltpu.CompilerParams(vmem_limit_bytes=VMEM_BYTES),
        cost_estimate=pl.CostEstimate(flops=2**22, bytes_accessed=64 * 2**20, transcendentals=0),
        name="roll_probe",
    )(offset, probe)


def times_i(pair):
    return -pair[1], pair[0]


def add(one, two):
    return one[0] + two[0], one[1] + two[1]


def sub(one, two):
    return one[0] - two[0], one[1] - two[1]


def butterfly(x0, x1, x2, x3, sign):
    even_sum, even_diff = add(x0, x2), sub(x0, x2)
    odd_sum, odd_diff = add(x1, x3), sub(x1, x3)
    turned = times_i(odd_diff)
    if sign < 0:
        first, third = sub(even_diff, turned), add(even_diff, turned)
    else:
        first, third = add(even_diff, turned), sub(even_diff, turned)
    return add(even_sum, odd_sum), first, sub(even_sum, odd_sum), third


def three_dots(left_high, left_low, right_high, right_low):
    total = jnp.dot(left_high, right_high, preferred_element_type=F32)
    total += jnp.dot(left_high, right_low, preferred_element_type=F32)
    total += jnp.dot(left_low, right_high, preferred_element_type=F32)
    return total


def strip_rows(core, z, y):
    start = core * (SIDE // 2) + lax.rem(z, 4) * (SIDE // 8) + lax.rem(y, 4) * STRIP
    return pl.ds(pl.multiple_of(start, STRIP), STRIP)


def main_kernel(
    offsets, tile_hbm, r0_hbm, r1_hbm, n0_hbm, n1_hbm, probe_hbm, binned_hbm, straight_hbm, turned_hbm, peak,
    change, sum_away, sum_kept,
    patch, wave, wide, mid_high, mid_low, full, tile, right, other, probe, binned, straight, turned, sems,
):
    r, _, y, z, core = my_place()
    position = lax.rem(r - core + ROWS, ROWS)
    o0, o1 = offsets[position, 0], offsets[position, 1]
    own_from = jnp.where(core == 1, 0, o0)
    own_to = jnp.where(core == 1, o0, SIDE)
    valid = jnp.where((core == 1) & (r == 0), 0, 1)
    quarters = [slice(QUARTER * a, QUARTER * (a + 1)) for a in range(4)]
    halves = [slice(0, QUARTER), slice(QUARTER, 2 * QUARTER)]

    early, late = [], []

    def fetch(group, source, target):
        copy = pltpu.make_async_copy(source, target, sems.at[len(early) + len(late)])
        copy.start()
        group.append(copy)

    for source0, source1, target in ((r0_hbm, r1_hbm, right), (n0_hbm, n1_hbm, other)):
        fetch(early, source0, target.at[:, :CUT])
        fetch(early, source1, target.at[:, CUT:])
    for piece in (slice(0, SIDE // 2), slice(SIDE // 2, SIDE)):
        fetch(early, tile_hbm.at[:, piece], tile.at[:, piece])
        fetch(early, probe_hbm.at[:, piece], probe.at[:, piece])
    fetch(late, straight_hbm, straight)
    fetch(late, turned_hbm, turned)
    fetch(late, binned_hbm, binned)
    step = QUARTER // 2
    for n in range(8):
        if n == 0:
            for k in (0, 2, 4, 5):
                early[k].wait()
        if n == 4:
            for k in (1, 3, 6, 7):
                early[k].wait()
        piece = slice(step * n, step * (n + 1))
        rows = lax.broadcasted_iota(jnp.int32, (step, SIDE), 0) + step * n
        cols = lax.broadcasted_iota(jnp.int32, (step, SIDE), 1)
        own = (rows >= own_from) & (rows < own_to)
        here = cols >= o1
        obj = []
        for part in range(2):
            mine = jnp.where(here, tile[part, piece, :], right[part, piece, :])
            mine = jnp.where(valid == 1, mine, 0.0)
            obj.append(jnp.where(own, mine, other[part, piece, :]))
            patch[part, piece, :] = obj[part]
        pr = probe[0, piece, :], probe[1, piece, :]
        wave[0, piece, :] = pr[0] * obj[0] - pr[1] * obj[1]
        wave[1, piece, :] = pr[0] * obj[1] + pr[1] * obj[0]
    for a in range(4):
        blocks = [(wave[0, quarters[a], quarters[b]], wave[1, quarters[a], quarters[b]]) for b in range(4)]
        for g, pair in enumerate(butterfly(*blocks, -1)):
            for part in range(2):
                mid_high[g, quarters[a], halves[part]], mid_low[g, quarters[a], halves[part]] = split_two(pair[part])

    late[0].wait()
    for g in range(4):
        out = three_dots(mid_high[g], mid_low[g], straight[g, 0], straight[g, 1])
        wide[0, :, quarters[g]] = out[:, :QUARTER]
        wide[1, :, quarters[g]] = out[:, QUARTER:]

    for b in range(4):
        blocks = [(wide[0, quarters[a], quarters[b]], wide[1, quarters[a], quarters[b]]) for a in range(4)]
        for h, pair in enumerate(butterfly(*blocks, -1)):
            for part in range(2):
                high, low = split_two(pair[part])
                full[h, 0, halves[part], quarters[b]] = high
                full[h, 1, halves[part], quarters[b]] = low

    late[1].wait()
    late[2].wait()
    for h in range(4):
        spec = three_dots(turned[h, 0], turned[h, 1], full[h, 0], full[h, 1])
        real, imag = spec[:QUARTER], spec[QUARTER:]
        power = real * real + imag * imag
        level = binned[:, 8 * h : 8 * h + 8, :].reshape(QUARTER, SIDE)
        factor = jnp.sqrt(level) * lax.rsqrt(jnp.maximum(power, 0.0625))
        for part, value in enumerate((real * factor, imag * factor)):
            high, low = split_two(value)
            full[h, 0, halves[part], :] = high
            full[h, 1, halves[part], :] = low

    for h in range(4):
        back = three_dots(straight[h, 0], straight[h, 1], full[h, 0], full[h, 1])
        wide[0, quarters[h], :] = back[:QUARTER]
        wide[1, quarters[h], :] = back[QUARTER:]

    for b in range(4):
        blocks = [(wide[0, quarters[h], quarters[b]], wide[1, quarters[h], quarters[b]]) for h in range(4)]
        for a, pair in enumerate(butterfly(*blocks, 1)):
            for part in range(2):
                mid_high[b, quarters[a], halves[part]], mid_low[b, quarters[a], halves[part]] = split_two(pair[part])

    for g in range(4):
        out = three_dots(mid_high[g], mid_low[g], turned[g, 0], turned[g, 1])
        wide[0, :, quarters[g]] = out[:, :QUARTER]
        wide[1, :, quarters[g]] = out[:, QUARTER:]

    scale = 1.0 / peak[0:1, 0:1]
    for a in range(4):
        blocks = [(wide[0, quarters[a], quarters[g]], wide[1, quarters[a], quarters[g]]) for g in range(4)]
        for b, back in enumerate(butterfly(*blocks, 1)):
            at = (quarters[a], quarters[b])
            dr = back[0] - wave[0, at[0], at[1]]
            di = back[1] - wave[1, at[0], at[1]]
            pr, pi = probe[0, at[0], at[1]], probe[1, at[0], at[1]]
            change[0, at[0], at[1]] = (pr * dr + pi * di) * scale
            change[1, at[0], at[1]] = (pr * di - pi * dr) * scale
            cr, ci = patch[0, at[0], at[1]], patch[1, at[0], at[1]]
            wide[0, at[0], at[1]] = cr * dr + ci * di
            wide[1, at[0], at[1]] = cr * di - ci * dr
            wide[2, at[0], at[1]] = cr * cr + ci * ci

    up = lax.rem(SIDE - o0, SIDE)
    left = lax.rem(SIDE - o1, SIDE)
    for part in range(3):
        wide[part] = roll_both(wide[part], up, left)
        for i in range(4):
            for j in range(4):
                sum_kept[i, j, part] = wide[part, strip_rows(core, z + i, y + j), :]
                sum_away[i, j, part] = wide[part, strip_rows(1 - core, z + i, y + j), :]


def main_call(offsets, tile, rights, others, probe, binned, peak):
    straight, turned = dft_tables()
    whole = (2, SIDE, SIDE)
    half = (4, 4, 3, STRIP, SIDE)
    vmem = pl.BlockSpec(memory_space=pltpu.VMEM)
    anywhere = pl.BlockSpec(memory_space=pl.ANY)
    tables = (4, 2, 2 * QUARTER, 2 * QUARTER)
    return pl.pallas_call(
        main_kernel,
        out_shape=[jax.ShapeDtypeStruct(s, F32) for s in (whole, half, half)],
        in_specs=[pl.BlockSpec(memory_space=pltpu.SMEM)] + [anywhere] * 9 + [vmem],
        out_specs=[vmem] * 3,
        scratch_shapes=[
            pltpu.VMEM(whole, F32),
            pltpu.VMEM(whole, F32),
            pltpu.VMEM((3, SIDE, SIDE), F32),
            pltpu.VMEM((4, SIDE, 2 * QUARTER), BF16),
            pltpu.VMEM((4, SIDE, 2 * QUARTER), BF16),
            pltpu.VMEM((4, 2, 2 * QUARTER, SIDE), BF16),
            pltpu.VMEM(whole, F32),
            pltpu.VMEM(whole, F32),
            pltpu.VMEM(whole, F32),
            pltpu.VMEM(whole, F32),
            pltpu.VMEM((ROWS, 32, SIDE), F32),
            pltpu.VMEM(tables, BF16),
            pltpu.VMEM(tables, BF16),
            pltpu.SemaphoreType.DMA((11,)),
        ],
        compiler_params=pltpu.CompilerParams(vmem_limit_bytes=VMEM_BYTES),
        cost_estimate=pl.CostEstimate(flops=8 * 2**30, bytes_accessed=20 * 2**20, transcendentals=2**19),
        name="phase_update",
    )(offsets, tile, *rights, *others, probe, binned, jnp.asarray(straight), jnp.asarray(turned), peak)


def send(block, axis, route):
    return lax.ppermute(block, axis, route)


def device_pairs(move):
    pairs = []
    for r in range(ROWS):
        for p in range(COLS):
            target = move(r, p)
            if target is not None:
                pairs.append((r * COLS + p, target[0] * COLS + target[1]))
    return pairs


def gather_pairs(r, p):
    if p % 2 == 0:
        return (r - 1, p) if r > 0 else None
    return ((r + 1) % ROWS, p)


def scatter_pairs(r, p):
    if p % 2 == 0:
        return (r + 1, p) if r < ROWS - 1 else None
    return ((r - 1) % ROWS, p)


def ring_z(distance):
    return [(p, (p + 2 * distance) % COLS) for p in range(COLS)]


def ring_y(distance):
    return [(r, (r + 4 * distance) % ROWS) for r in range(ROWS)]


def ring_x(distance):
    return [(r, r // 4 * 4 + (r + distance) % 4) for r in range(ROWS)]


def around(values, axis, ring):
    return [send(values, axis, ring(k)) for k in (1, 2, 3)]


def scatter_sum(values, axis, ring):
    first, second, third = (send(values[k], axis, ring(k)) for k in (1, 2, 3))
    return (values[0] + second) + (first + third)


def place_kernel(mine, *refs):
    _, _, y, z, core = my_place()
    pieces, out, rows, sem = refs[:4], refs[-3], refs[-2], refs[-1]
    half = core if mine else 1 - core
    for i in range(4):
        for j in range(4):
            strip = strip_rows(0, z + 4 - i, y + 4 - j)
            for part in range(2):
                rows[part, strip, :] = pieces[i][j, part] if mine else refs[0][i, j, part]
    target = out.at[:, pl.ds(pl.multiple_of(half * (SIDE // 2), SIDE // 2), SIDE // 2), :]
    copy = pltpu.make_async_copy(rows, target, sem)
    copy.start()
    copy.wait()


def place_strips(mine, arrays):
    anywhere = pl.BlockSpec(memory_space=pl.ANY)
    vmem = pl.BlockSpec(memory_space=pltpu.VMEM)
    return pl.pallas_call(
        functools.partial(place_kernel, mine),
        out_shape=jax.ShapeDtypeStruct((2, SIDE, SIDE), F32),
        in_specs=[vmem] * 4 if mine else [vmem, anywhere],
        out_specs=anywhere,
        input_output_aliases={} if mine else {1: 0},
        scratch_shapes=[pltpu.VMEM((2, SIDE // 2, SIDE), F32), pltpu.SemaphoreType.DMA(())],
        compiler_params=pltpu.CompilerParams(vmem_limit_bytes=VMEM_BYTES),
        cost_estimate=pl.CostEstimate(flops=0, bytes_accessed=2 * 2**20, transcendentals=0),
        name="place_mine" if mine else "place_other",
    )(*arrays)


def on_device(frames, dark, gain, offsets, object_field, probe):
    r = lax.axis_index("readout")
    p = lax.axis_index("pos")
    flip = lax.rem(p, 2)
    z = p // 2
    x, y = lax.rem(r, 4), r // 4
    position = lax.rem(r - flip + ROWS, ROWS)
    beside = lax.rem(r - 1 + flip + ROWS, ROWS)
    o1 = offsets[position, 1]
    o1_beside = offsets[beside, 1]

    to_left = [(i, i - 1) for i in range(1, COLS)]
    to_right = [(i, i + 1) for i in range(COLS - 1)]
    swap_cores = [(i, i ^ 1) for i in range(COLS)]
    half = SIDE // 2
    chunks = [object_field[:, :CUT], object_field[:, CUT:]]
    chunks = lax.optimization_barrier(chunks)
    rights = [send(chunk, "pos", to_left) for chunk in chunks]
    binned = bin_frames(frames, dark, gain)
    cols = lax.broadcasted_iota(jnp.int32, (2, SIDE, SIDE), 2)
    regrouped = lax.all_to_all(binned, "readout", split_axis=0, concat_axis=0, tiled=True)
    joined = []
    for a in range(2):
        before = (joined[0], regrouped) if a > 0 else binned
        rights[a], _ = lax.optimization_barrier((rights[a], before))
        joined.append(jnp.where(cols[:, : chunks[a].shape[1]] >= o1_beside, chunks[a], rights[a]))
    others = [send(block, BOTH, device_pairs(gather_pairs)) for block in joined]
    rolled, peak = roll_probe(offsets, probe)

    change, sum_away, sum_kept = main_call(offsets, object_field, rights, others, rolled, regrouped, peak)

    rows = lax.broadcasted_iota(jnp.int32, (2, SIDE, SIDE), 1)
    upper, upper_beside = rows >= offsets[position, 0], rows >= offsets[beside, 0]
    mine = ((flip == 0) & upper) | ((flip == 1) & (r > 0) & ~upper)
    theirs = ((flip == 0) & ~upper_beside) | ((flip == 1) & upper_beside)

    def landing(inside, inside_beside):
        return jnp.where(mine & inside, change, 0.0) + jnp.where(theirs & inside_beside, arrived, 0.0)

    arrived = send(change, BOTH, device_pairs(scatter_pairs))
    total = sum_kept + send(sum_away, "pos", swap_cores)
    total = scatter_sum(total, "pos", ring_z)
    total, arrived = lax.optimization_barrier((total, arrived))
    total, outward = lax.optimization_barrier((total, landing(cols < o1, cols < o1_beside)))
    landed = send(outward, "pos", to_right)
    total = scatter_sum(total, "readout", ring_y)
    first, second, third = around(total, "readout", ring_x)
    total = (total + second) + (first + third)
    start = flip * half + z * (SIDE // 8) + y * STRIP
    piece = lax.dynamic_slice_in_dim(probe, start, STRIP, 1) + total[:2] / total[2:]
    strips = jnp.stack([piece] + around(piece, "readout", ring_y))
    change, arrived, _ = lax.optimization_barrier((change, arrived, strips))
    inward = object_field + landing(cols >= o1, cols >= o1_beside)
    own = [strips] + around(strips, "pos", ring_z)
    object_new = inward + landed
    own, object_new = lax.optimization_barrier((own, object_new))
    other = send(jnp.stack(own), "pos", swap_cores)
    probe_new = place_strips(False, [other, place_strips(True, own)])
    return (object_new, probe_new)


def solution(mesh):
    in_specs = (
        P("pos", "readout", None),
        P("readout", None),
        P("readout", None),
        P("pos", None),
        P(None, "readout", "pos"),
        P(),
    )
    out_specs = (P(None, "readout", "pos"), P())
    return jax.shard_map(
        on_device, mesh=mesh, in_specs=in_specs, out_specs=out_specs, check_vma=False
    )
```
